32 devices in a mesh: segment: 4 (over x, core), ctx: 4 (over z), head: 2 (over y).
Axes of the slice: x: 2, y: 2, z: 4, core: 2. Of those that a mesh axis runs over, the one named last changes fastest.
Arguments:
- queries: bfloat16 [512, 8192], P('segment', 'head'), may hold values from -6 to 6
- keys: bfloat16 [65536, 1024], P(('segment', 'ctx'), 'head'), may hold values from -6 to 6
- values: bfloat16 [65536, 1024], P(('segment', 'ctx'), 'head'), may hold values from -6 to 6
- lengths: int32 [4], P('segment'), may hold values from 6145 to 16384, as said below
- selected: int32 [4, 3], P('segment'), may hold values from 0 to 7, as said below
- out_weight: bfloat16 [8192, 8192], P(('head', 'ctx')), may hold values from -3 to 3
Outputs:
- handed: bfloat16 [512, 8192], P('segment', ('head', 'ctx'))
The draws below stay inside these ranges and needn't reach their ends.
Inputs may be any that keep to these rules, and one draw needn't show every extreme that they name: `lengths`: Even-indexed sections hold 8192 cached positions or fewer, odd-indexed ones more than 8192; some section holds exactly 16384. `selected`: each row names 3 distinct blocks, each holding at least one cached position of its section; block 0 and the block holding the section's last cached position are always named.
All inputs are finite; a program needn't handle non-finite values.
Results may differ from the reference program's by a relative error of at most 0.019.
Values may be sent and summed in bfloat16 or wider, within the bound.
A program may use at most 192 MiB of HBM per device.

```python
import math
import jax
import jax.numpy as jnp
from jax import lax

D = 8192
QUERY_HEADS = 64
KV_HEADS_COUNT = 8
HEAD_DIM = 128
SLICE_ROWS = 128
BLOCK = 2048
SEL = 3
LIGHT = 8192
SECTION_CACHE = 16384
QROWS = 512
ALL_CACHE_ROWS = 65536
N_SEGMENT = 4


def lengths_and_blocks(key):
    base = jax.random.fold_in(key, 11)
    key_light, key_heavy, key_full, key_rank = jax.random.split(base, 4)
    section_count = QROWS // SLICE_ROWS
    segment_ids = jnp.arange(section_count, dtype=jnp.int32)
    light = jax.random.randint(key_light, (section_count,), SEL * BLOCK + 1, LIGHT + 1)
    heavy = jax.random.randint(key_heavy, (section_count,), LIGHT + 1, SECTION_CACHE + 1)
    full_at = 2 * jax.random.randint(key_full, (), 0, section_count // 2) + 1
    cached = jnp.where(segment_ids % 2 == 1, heavy, light)
    cached = jnp.where(segment_ids == full_at, SECTION_CACHE, cached).astype(jnp.int32)
    block_count = SECTION_CACHE // BLOCK
    last_block = (cached - 1) // BLOCK
    ranks = jax.vmap(lambda sub: jax.random.permutation(sub, block_count))(jax.random.split(key_rank, section_count))
    block_ids = jnp.arange(block_count, dtype=jnp.int32)[None, :]
    inside = (block_ids >= 1) & (block_ids < last_block[:, None])
    score = jnp.where(inside, ranks.astype(jnp.int32), block_count + block_ids)
    order = jnp.argsort(score, axis=1, stable=True)[:, :SEL - 2].astype(jnp.int32)
    chosen = jnp.concatenate([jnp.zeros((section_count, 1), jnp.int32), order, last_block[:, None].astype(jnp.int32)], axis=1)
    return (cached, chosen.astype(jnp.int32))


def draw_lengths(key, part):
    return lengths_and_blocks(key)[0]


def draw_selected(key, part):
    return lengths_and_blocks(key)[1]


def draw_queries(key, part):
    inner_function = jax.random.fold_in(key, 31)
    sampled_blocks = jnp.clip(jax.random.normal(inner_function, (QROWS, QUERY_HEADS * HEAD_DIM), jnp.float32), -5.0, 5.0)
    return sampled_blocks.astype(jnp.bfloat16)


def draw_keys(key, part):
    inner_function = jax.random.fold_in(key, 37)
    sampled_blocks = jnp.clip(jax.random.normal(inner_function, (ALL_CACHE_ROWS, KV_HEADS_COUNT * HEAD_DIM), jnp.float32), -5.0, 5.0)
    return sampled_blocks.astype(jnp.bfloat16)


def block_levels(stream_key, shape, cuts, least, largest):
    def one(dim, parts):
        steps = jax.random.uniform(jax.random.fold_in(jax.random.fold_in(stream_key, 6), dim), (parts,), jnp.float32, least / len(cuts), largest / len(cuts))
        return jnp.repeat(jnp.exp(steps), shape[dim] // parts).reshape((-1,) + (1,) * (len(shape) - dim - 1))

    level = one(*cuts[0])
    for cut in cuts[1:]:
        level = level * one(*cut)
    return level


def centred(key, extent, deviation, bound, pieces=(), held_as=jnp.bfloat16):
    values = jax.random.normal(key, extent, jnp.float32) * deviation
    if len(pieces) > 0:
        values = block_levels(key, extent, pieces, -0.22, 0.18) * values
    return jnp.clip(values, min=-bound, max=bound).astype(held_as)


def setup_inputs(seed: int = 0) -> dict:
    splits = jax.random.split(jax.random.key(seed), 7)
    queries = draw_queries(jax.random.fold_in(splits[6], 71), 0)
    keys = draw_keys(jax.random.fold_in(splits[6], 71), 0)
    values = centred(splits[2], (ALL_CACHE_ROWS, KV_HEADS_COUNT * HEAD_DIM), 1.0, 6.0, ((0, 16), (1, 2)))
    lengths = draw_lengths(jax.random.fold_in(splits[6], 71), 0)
    selected = draw_selected(jax.random.fold_in(splits[6], 71), 0)
    out_weight = centred(splits[5], (QUERY_HEADS * HEAD_DIM, D), 0.5, 3.0, ((0, 8),))
    return {"queries": queries, "keys": keys, "values": values, "lengths": lengths, "selected": selected, "out_weight": out_weight}


MASKED = -1e+30

def reference(queries, keys, values, lengths, selected, out_weight):
    heads_per_group = QUERY_HEADS // KV_HEADS_COUNT
    score_scale = 1.0 / math.sqrt(HEAD_DIM)
    every_query = queries.reshape(N_SEGMENT, SLICE_ROWS, KV_HEADS_COUNT, heads_per_group, HEAD_DIM)
    every_key = keys.reshape(N_SEGMENT, SECTION_CACHE, KV_HEADS_COUNT, HEAD_DIM)
    every_value = values.reshape(N_SEGMENT, SECTION_CACHE, KV_HEADS_COUNT, HEAD_DIM)

    def one_segment(segment_args):
        query_part, key_part, value_part, length, chosen = segment_args
        positions = (chosen[:, None] * BLOCK + jnp.arange(BLOCK, dtype=jnp.int32)[None, :]).reshape(-1).astype(jnp.int32)
        usable = positions < length
        key_sel = key_part[positions]
        value_sel = value_part[positions]

        def one_head(head_args):
            query_head, key_head, value_head = head_args
            scores = jnp.einsum('rgd,pd->rgp', query_head.astype(jnp.float32), key_head.astype(jnp.float32)) * score_scale
            scores = jnp.where(usable[None, None, :], scores, MASKED)
            top = lax.optimization_barrier(jnp.max(scores, axis=-1, keepdims=True))
            expo = jnp.where(usable[None, None, :], jnp.exp(scores - top), 0.0)
            total = lax.optimization_barrier(jnp.sum(expo, axis=-1))
            weights = lax.optimization_barrier(expo.astype(jnp.bfloat16))
            summed = jnp.einsum('rgp,pd->rgd', weights.astype(jnp.float32), value_head.astype(jnp.float32))
            return (summed / total[..., None]).astype(jnp.bfloat16)
        heads_out = lax.map(one_head, (query_part.transpose(1, 0, 2, 3), key_sel.transpose(1, 0, 2), value_sel.transpose(1, 0, 2)))
        attention = heads_out.transpose(1, 0, 2, 3).reshape(SLICE_ROWS, QUERY_HEADS * HEAD_DIM)
        return jnp.dot(attention, out_weight, preferred_element_type=jnp.float32)
    projected = lax.map(one_segment, (every_query, every_key, every_value, lengths, selected))
    handed = jnp.roll(projected, 1, axis=0).astype(jnp.bfloat16)
    return handed.reshape(N_SEGMENT * SLICE_ROWS, D)
```

```python
import functools
import math

import jax
import jax.numpy as jnp
from jax import lax
from jax.experimental import pallas as pl
from jax.experimental.pallas import tpu as pltpu
from jax.sharding import PartitionSpec as P

HEAD_DIM = 128
BLOCK = 2048
MASKED = -1e30
FLOOR = -1e20
UNITS = math.log2(math.e) / math.sqrt(HEAD_DIM)
MESH = pl.DeviceIdType.MESH


def relay(
    sizes,
    length_ref,
    chosen_ref,
    q_hbm,
    k_hbm,
    v_hbm,
    w_hbm,
    out_ref,
    q_buf,
    k_buf,
    v_buf,
    w_buf,
    bias,
    a_send,
    a_recv,
    t_send,
    t_recv,
    attn,
    y_send,
    y_recv,
    z_send,
    z_recv,
    load_sem,
    k_sem,
    v_sem,
    a_sems,
    t_sems,
    y_sems,
    z_sems,
):
    S, C, H = sizes
    seg, ctx, head = lax.axis_index("segment"), lax.axis_index("ctx"), lax.axis_index("head")
    rows, q_cols = q_buf.shape
    kv_count, span, _ = k_buf.shape
    per_ctx = q_cols // (HEAD_DIM * C)
    group = q_cols // (HEAD_DIM * kv_count)
    together = 2 if per_ctx % 2 == 0 else 1
    width = out_ref.shape[1]
    stat_rows = t_send.shape[1]
    aligned = kv_count == C

    barrier = pltpu.get_barrier_semaphore()

    def greet(s, c, h):
        pl.semaphore_signal(barrier, inc=1, device_id=(s, c, h), device_id_type=MESH)

    for k in range(1, C):
        greet(seg, lax.rem(ctx + k, C), head)
    for k in range(1, H):
        greet(seg, ctx, lax.rem(head + k, H))
    for k in range(C):
        greet(lax.rem(seg + S - 1, S), lax.rem(ctx + k, C), head)

    def load_q():
        return pltpu.make_async_copy(q_hbm, q_buf, load_sem.at[0])

    def load_w():
        return pltpu.make_async_copy(w_hbm, w_buf, load_sem.at[1])

    def load_kv(i):
        which = lax.rem(ctx + 1 + i, C) if aligned else i
        columns = pl.ds(pl.multiple_of(which * HEAD_DIM, HEAD_DIM), HEAD_DIM)
        return (
            pltpu.make_async_copy(k_hbm.at[:, columns], k_buf.at[i], k_sem.at[i]),
            pltpu.make_async_copy(v_hbm.at[:, columns], v_buf.at[i], v_sem.at[i]),
        )

    load_q().start()
    for i in range(kv_count):
        for copy in load_kv(i):
            copy.start()
    load_w().start()

    length = length_ref[0]
    for b in range(span // BLOCK):
        first = ctx * span + b * BLOCK
        picked = jnp.int32(0)
        for i in range(chosen_ref.shape[1]):
            picked = jnp.where(chosen_ref[0, i] == first // BLOCK, 1, picked)
        limit = jnp.where(picked == 1, length, 0)
        place = first + lax.broadcasted_iota(jnp.int32, (8, BLOCK), 1)
        bias[:, b * BLOCK : (b + 1) * BLOCK] = jnp.where(place < limit, 0.0, MASKED)

    load_q().wait()
    if not aligned:
        for i in range(kv_count):
            for copy in load_kv(i):
                copy.wait()

    def a_copies(k):
        to = (seg, lax.rem(ctx + 1 + k, C), head)
        return (
            pltpu.make_async_remote_copy(
                src_ref=a_send.at[k], dst_ref=a_recv.at[k], send_sem=a_sems.at[0, k],
                recv_sem=a_sems.at[1, k], device_id=to, device_id_type=MESH,
            ),
            pltpu.make_async_remote_copy(
                src_ref=t_send.at[k], dst_ref=t_recv.at[k], send_sem=t_sems.at[0, k],
                recv_sem=t_sems.at[1, k], device_id=to, device_id_type=MESH,
            ),
        )

    lane = lax.broadcasted_iota(jnp.int32, (rows, HEAD_DIM), 1)

    def unit(k, carry):
        owner = lax.rem(ctx + 1 + k, C)
        if aligned:
            slot = k
            for copy in load_kv(k):
                copy.wait()
        else:
            slot = (owner * per_ctx) // group

        def heads(t, stats):
            at = pl.multiple_of((owner * per_ctx + t * together) * HEAD_DIM, HEAD_DIM)
            q = jnp.concatenate(
                [
                    q_buf[:, pl.ds(pl.multiple_of(at + i * HEAD_DIM, HEAD_DIM), HEAD_DIM)]
                    for i in range(together)
                ],
                axis=0,
            )
            scores = lax.dot_general(
                q, k_buf[slot], (((1,), (1,)), ((), ())), preferred_element_type=jnp.float32
            )
            scores = scores + bias[0:1, :]
            top = jnp.maximum(jnp.max(scores, axis=1, keepdims=True), FLOOR)
            expo = jnp.exp2(scores * UNITS - top * UNITS).astype(jnp.bfloat16)
            ones = jnp.ones((span, HEAD_DIM), jnp.bfloat16)
            summed = jnp.dot(
                expo,
                jnp.concatenate([v_buf[slot], ones], axis=1),
                preferred_element_type=jnp.float32,
            )
            for i in range(together):
                part = slice(i * rows, (i + 1) * rows)
                j = t * together + i
                dst = pl.multiple_of(j * HEAD_DIM, HEAD_DIM)
                a_send[k, :, pl.ds(dst, HEAD_DIM)] = summed[part, :HEAD_DIM].astype(jnp.bfloat16)
                stats = jnp.where(lane == j, top[part], stats)
                stats = jnp.where(lane == per_ctx + j, summed[part, HEAD_DIM:], stats)
            return stats

        stats = lax.fori_loop(
            0, per_ctx // together, heads, jnp.zeros((rows, HEAD_DIM), jnp.float32)
        )
        t_send[k] = jnp.transpose(stats)[:stat_rows]

        @pl.when(k == 0)
        def _():
            pl.semaphore_wait(barrier, 2 * C + H - 2)

        @pl.when(k < C - 1)
        def _():
            for copy in a_copies(k):
                copy.start()

        return carry

    lax.fori_loop(0, C, unit, 0)

    for k in range(C - 1):
        for copy in a_copies(k):
            copy.wait()
    load_w().wait()

    def column_form(block):
        fill = jnp.zeros((HEAD_DIM - stat_rows, rows), jnp.float32)
        return jnp.transpose(jnp.concatenate([block, fill], axis=0))

    stats = [column_form(t_recv[k]) for k in range(C - 1)] + [column_form(t_send[C - 1])]
    tops = [s[:, :per_ctx] for s in stats]
    sums = [s[:, per_ctx : 2 * per_ctx] for s in stats]
    largest = functools.reduce(jnp.maximum, tops)
    factors = [jnp.exp2((top - largest) * UNITS) for top in tops]
    total = functools.reduce(jnp.add, [f * s for f, s in zip(factors, sums)])
    factors = [f / total for f in factors]
    for j in range(per_ctx):
        part = slice(j * HEAD_DIM, (j + 1) * HEAD_DIM)
        shares = [a_recv[k, :, part] for k in range(C - 1)] + [a_send[C - 1, :, part]]
        joined = functools.reduce(
            jnp.add,
            [f[:, j : j + 1] * share.astype(jnp.float32) for f, share in zip(factors, shares)],
        )
        attn[:, part] = joined.astype(jnp.bfloat16)

    def columns_of(h, k):
        c = lax.rem(ctx + 1 + k, C)
        start = pl.multiple_of((h * C + c) * width, width)
        return jnp.dot(attn[...], w_buf[:, pl.ds(start, width)], preferred_element_type=jnp.float32)

    def y_copy(i, k):
        return pltpu.make_async_remote_copy(
            src_ref=y_send.at[i, k], dst_ref=y_recv.at[i, k], send_sem=y_sems.at[0, i, k],
            recv_sem=y_sems.at[1, i, k], device_id=(seg, ctx, lax.rem(head + 1 + i, H)),
            device_id_type=MESH,
        )

    def z_copy(k):
        return pltpu.make_async_remote_copy(
            src_ref=z_send.at[k], dst_ref=z_recv.at[k], send_sem=z_sems.at[0, k],
            recv_sem=z_sems.at[1, k],
            device_id=(lax.rem(seg + 1, S), lax.rem(ctx + 1 + k, C), head),
            device_id_type=MESH,
        )

    def outgoing(n, carry):
        k, i = n // (H - 1), n % (H - 1)
        y_send[i, k] = columns_of(lax.rem(head + 1 + i, H), k).astype(jnp.bfloat16)
        y_copy(i, k).start()
        return carry

    lax.fori_loop(0, C * (H - 1), outgoing, 0)

    def passed_on(k, carry):
        mine = columns_of(head, k)
        for i in range(H - 1):
            y_copy(i, k).wait()
            mine = mine + y_recv[i, k].astype(jnp.float32)
        z_send[k] = mine.astype(jnp.bfloat16)
        z_copy(k).start()
        return carry

    lax.fori_loop(0, C, passed_on, 0)

    result = jnp.zeros(out_ref.shape, jnp.float32)
    for k in range(C):
        z_copy(k).wait()
        result = result + z_recv[k].astype(jnp.float32)
    out_ref[...] = result.astype(out_ref.dtype)


def on_device(queries, keys, values, lengths, selected, out_weight):
    S, C, H = lax.axis_size("segment"), lax.axis_size("ctx"), lax.axis_size("head")
    rows, q_cols = queries.shape
    span, kv_cols = keys.shape
    kv_count = kv_cols // HEAD_DIM
    depth, d = out_weight.shape
    width = d // (C * H)
    stat_rows = -(-2 * (depth // HEAD_DIM) // 8) * 8
    whole = pl.BlockSpec(memory_space=pl.ANY)
    scalars = pl.BlockSpec(memory_space=pltpu.SMEM)
    wire = jnp.bfloat16
    return pl.pallas_call(
        functools.partial(relay, (S, C, H)),
        out_shape=jax.ShapeDtypeStruct((rows, width), jnp.bfloat16),
        in_specs=[scalars, scalars, whole, whole, whole, whole],
        out_specs=pl.BlockSpec(memory_space=pltpu.VMEM),
        scratch_shapes=[
            pltpu.VMEM((rows, q_cols), queries.dtype),
            pltpu.VMEM((kv_count, span, HEAD_DIM), keys.dtype),
            pltpu.VMEM((kv_count, span, HEAD_DIM), values.dtype),
            pltpu.VMEM((depth, d), out_weight.dtype),
            pltpu.VMEM((8, span), jnp.float32),
            pltpu.VMEM((C, rows, depth), wire),
            pltpu.VMEM((C - 1, rows, depth), wire),
            pltpu.VMEM((C, stat_rows, rows), jnp.float32),
            pltpu.VMEM((C - 1, stat_rows, rows), jnp.float32),
            pltpu.VMEM((rows, depth), wire),
            pltpu.VMEM((H - 1, C, rows, width), wire),
            pltpu.VMEM((H - 1, C, rows, width), wire),
            pltpu.VMEM((C, rows, width), wire),
            pltpu.VMEM((C, rows, width), wire),
            pltpu.SemaphoreType.DMA((2,)),
            pltpu.SemaphoreType.DMA((kv_count,)),
            pltpu.SemaphoreType.DMA((kv_count,)),
            pltpu.SemaphoreType.DMA((2, C - 1)),
            pltpu.SemaphoreType.DMA((2, C - 1)),
            pltpu.SemaphoreType.DMA((2, H - 1, C)),
            pltpu.SemaphoreType.DMA((2, C)),
        ],
        compiler_params=pltpu.CompilerParams(
            collective_id=0, has_side_effects=True, vmem_limit_bytes=58 * 2**20
        ),
        cost_estimate=pl.CostEstimate(
            flops=4 * rows * q_cols * span + 2 * rows * depth * d,
            bytes_accessed=2 * (rows * q_cols + 2 * span * kv_cols + depth * d),
            transcendentals=rows * q_cols // HEAD_DIM * span,
        ),
    )(lengths, selected, queries, keys, values, out_weight)


def solution(mesh):
    placed = (
        P("segment", "head"),
        P(("segment", "ctx"), "head"),
        P(("segment", "ctx"), "head"),
        P("segment"),
        P("segment", None),
        P(("head", "ctx"), None),
    )
    return jax.shard_map(
        on_device,
        mesh=mesh,
        in_specs=placed,
        out_specs=P("segment", ("head", "ctx")),
        check_vma=False,
    )
```

```python
import functools
import math

import jax
import jax.numpy as jnp
from jax import lax
from jax.experimental import pallas as pl
from jax.experimental.pallas import tpu as pltpu
from jax.sharding import PartitionSpec as P

HEAD_DIM = 128
BLOCK = 2048
MASKED = -1e30
FLOOR = -1e20
UNITS = math.log2(math.e) / math.sqrt(HEAD_DIM)
MESH = pl.DeviceIdType.MESH


def relay(
    sizes,
    length_ref,
    chosen_ref,
    q_hbm,
    k_hbm,
    v_hbm,
    w_hbm,
    out_ref,
    q_buf,
    k_buf,
    v_buf,
    w_buf,
    bias,
    a_send,
    a_recv,
    t_send,
    t_recv,
    attn,
    y_send,
    y_recv,
    z_send,
    z_recv,
    load_sem,
    k_sem,
    v_sem,
    a_sems,
    t_sems,
    y_sems,
    z_sems,
):
    S, C, H = sizes
    seg, ctx, head = lax.axis_index("segment"), lax.axis_index("ctx"), lax.axis_index("head")
    rows, q_cols = q_buf.shape
    kv_count, span, _ = k_buf.shape
    per_ctx = q_cols // (HEAD_DIM * C)
    group = q_cols // (HEAD_DIM * kv_count)
    together = math.gcd(per_ctx, 4)
    half = rows // 2
    width = out_ref.shape[1]
    stat_rows = t_send.shape[2]
    aligned = kv_count == C

    barrier = pltpu.get_barrier_semaphore()

    def greet(s, c, h):
        pl.semaphore_signal(barrier, inc=1, device_id=(s, c, h), device_id_type=MESH)

    for k in range(1, C):
        greet(seg, lax.rem(ctx + k, C), head)
    for k in range(1, H):
        greet(seg, ctx, lax.rem(head + k, H))
    for k in range(C):
        greet(lax.rem(seg + S - 1, S), lax.rem(ctx + k, C), head)

    def load_q():
        return pltpu.make_async_copy(q_hbm, q_buf, load_sem.at[0])

    def load_w():
        return pltpu.make_async_copy(w_hbm, w_buf, load_sem.at[1])

    def load_kv(i):
        which = lax.rem(ctx + 1 + i, C) if aligned else i
        columns = pl.ds(pl.multiple_of(which * HEAD_DIM, HEAD_DIM), HEAD_DIM)
        return (
            pltpu.make_async_copy(k_hbm.at[:, columns], k_buf.at[i], k_sem.at[i]),
            pltpu.make_async_copy(v_hbm.at[:, columns], v_buf.at[i], v_sem.at[i]),
        )

    load_q().start()
    for i in range(kv_count):
        for copy in load_kv(i):
            copy.start()
    load_w().start()

    length = length_ref[0]
    for b in range(span // BLOCK):
        first = ctx * span + b * BLOCK
        picked = jnp.int32(0)
        for i in range(chosen_ref.shape[1]):
            picked = jnp.where(chosen_ref[0, i] == first // BLOCK, 1, picked)
        limit = jnp.where(picked == 1, length, 0)
        place = first + lax.broadcasted_iota(jnp.int32, (8, BLOCK), 1)
        bias[:, b * BLOCK : (b + 1) * BLOCK] = jnp.where(place < limit, 0.0, MASKED)

    load_q().wait()
    if not aligned:
        for i in range(kv_count):
            for copy in load_kv(i):
                copy.wait()

    def a_copies(g, k):
        to = (seg, lax.rem(ctx + 1 + k, C), head)
        return (
            pltpu.make_async_remote_copy(
                src_ref=a_send.at[g, k], dst_ref=a_recv.at[g, k], send_sem=a_sems.at[0, g, k],
                recv_sem=a_sems.at[1, g, k], device_id=to, device_id_type=MESH,
            ),
            pltpu.make_async_remote_copy(
                src_ref=t_send.at[g, k], dst_ref=t_recv.at[g, k], send_sem=t_sems.at[0, g, k],
                recv_sem=t_sems.at[1, g, k], device_id=to, device_id_type=MESH,
            ),
        )

    lane = lax.broadcasted_iota(jnp.int32, (half, HEAD_DIM), 1)

    def unit(g, k):
        owner = lax.rem(ctx + 1 + k, C)
        slot = k if aligned else (owner * per_ctx) // group
        own_rows = pl.ds(pl.multiple_of(g * half, half), half)
        tiles = per_ctx // together
        scores = []
        for t in range(tiles):
            q = jnp.concatenate(
                [
                    q_buf[
                        own_rows,
                        pl.ds(
                            pl.multiple_of(
                                (owner * per_ctx + t * together + i) * HEAD_DIM, HEAD_DIM
                            ),
                            HEAD_DIM,
                        ),
                    ]
                    for i in range(together)
                ],
                axis=0,
            )
            scores.append(
                lax.dot_general(
                    q, k_buf[slot], (((1,), (1,)), ((), ())), preferred_element_type=jnp.float32
                )
                + bias[0:1, :]
            )
        stats = jnp.zeros((half, HEAD_DIM), jnp.float32)
        for t in range(tiles):
            top = jnp.maximum(jnp.max(scores[t], axis=1, keepdims=True), FLOOR)
            expo = jnp.exp2(scores[t] * UNITS - top * UNITS).astype(jnp.bfloat16)
            ones = jnp.ones((span, HEAD_DIM), jnp.bfloat16)
            summed = jnp.dot(
                expo,
                jnp.concatenate([v_buf[slot], ones], axis=1),
                preferred_element_type=jnp.float32,
            )
            for i in range(together):
                part = slice(i * half, (i + 1) * half)
                j = t * together + i
                a_send[g, k, :, j * HEAD_DIM : (j + 1) * HEAD_DIM] = summed[
                    part, :HEAD_DIM
                ].astype(jnp.bfloat16)
                stats = jnp.where(lane == j, top[part], stats)
                stats = jnp.where(lane == per_ctx + j, summed[part, HEAD_DIM:], stats)
        fill = jnp.zeros((HEAD_DIM - half, HEAD_DIM), jnp.float32)
        t_send[g, k] = jnp.transpose(jnp.concatenate([stats, fill], axis=0))[:stat_rows]

    def column_form(block):
        fill = jnp.zeros((HEAD_DIM - stat_rows, HEAD_DIM), jnp.float32)
        return jnp.transpose(jnp.concatenate([block, fill], axis=0))[:half]

    def combine(g):
        for k in range(C - 1):
            for copy in a_copies(g, k):
                copy.wait()
        stats = [column_form(t_recv[g, k]) for k in range(C - 1)]
        stats.append(column_form(t_send[g, C - 1]))
        tops = [s[:, :per_ctx] for s in stats]
        sums = [s[:, per_ctx : 2 * per_ctx] for s in stats]
        largest = functools.reduce(jnp.maximum, tops)
        factors = [jnp.exp2((top - largest) * UNITS) for top in tops]
        total = functools.reduce(jnp.add, [f * s for f, s in zip(factors, sums)])
        factors = [f / total for f in factors]
        for j in range(per_ctx):
            part = slice(j * HEAD_DIM, (j + 1) * HEAD_DIM)
            shares = [a_recv[g, k, :, part] for k in range(C - 1)] + [a_send[g, C - 1, :, part]]
            joined = functools.reduce(
                jnp.add,
                [f[:, j : j + 1] * share.astype(jnp.float32) for f, share in zip(factors, shares)],
            )
            attn[g, :, part] = joined.astype(jnp.bfloat16)

    def columns_of(g, h, k):
        c = lax.rem(ctx + 1 + k, C)
        start = pl.multiple_of((h * C + c) * width, width)
        return jnp.dot(attn[g], w_buf[:, pl.ds(start, width)], preferred_element_type=jnp.float32)

    def y_copy(g, i, k):
        return pltpu.make_async_remote_copy(
            src_ref=y_send.at[g, i, k], dst_ref=y_recv.at[g, i, k], send_sem=y_sems.at[0, g, i, k],
            recv_sem=y_sems.at[1, g, i, k], device_id=(seg, ctx, lax.rem(head + 1 + i, H)),
            device_id_type=MESH,
        )

    def z_copy(g, k):
        return pltpu.make_async_remote_copy(
            src_ref=z_send.at[g, k], dst_ref=z_recv.at[g, k], send_sem=z_sems.at[0, g, k],
            recv_sem=z_sems.at[1, g, k],
            device_id=(lax.rem(seg + 1, S), lax.rem(ctx + 1 + k, C), head),
            device_id_type=MESH,
        )

    def outgoing(g):
        def step(n, carry):
            k, i = n // (H - 1), n % (H - 1)
            y_send[g, i, k] = columns_of(g, lax.rem(head + 1 + i, H), k).astype(jnp.bfloat16)
            y_copy(g, i, k).start()
            return carry

        lax.fori_loop(0, C * (H - 1), step, 0)

    def pass_on(g, first, last):
        def step(k, carry):
            mine = columns_of(g, head, k)
            for i in range(H - 1):
                y_copy(g, i, k).wait()
                mine = mine + y_recv[g, i, k].astype(jnp.float32)
            z_send[g, k] = mine.astype(jnp.bfloat16)
            z_copy(g, k).start()
            return carry

        lax.fori_loop(first, last, step, 0)

    def turn(n, carry):
        g, k = n // C, n % C
        if aligned:

            @pl.when(n < C)
            def _():
                for copy in load_kv(k):
                    copy.wait()

        unit(g, k)

        @pl.when(n == 0)
        def _():
            pl.semaphore_wait(barrier, 2 * C + H - 2)

        @pl.when(k < C - 1)
        def _():
            for copy in a_copies(g, k):
                copy.start()

        @pl.when(n == C)
        def _():
            load_w().wait()
            combine(0)
            outgoing(0)

        @pl.when(n > C)
        def _():
            pass_on(0, (k - 1) * C // (C - 1), k * C // (C - 1))

        return carry

    lax.fori_loop(0, 2 * C, turn, 0)
    combine(1)
    outgoing(1)
    pass_on(1, 0, C)

    for g in range(2):
        result = jnp.zeros((half, width), jnp.float32)
        for k in range(C):
            z_copy(g, k).wait()
            result = result + z_recv[g, k].astype(jnp.float32)
        out_ref[g * half : (g + 1) * half, :] = result.astype(out_ref.dtype)


def on_device(queries, keys, values, lengths, selected, out_weight):
    S, C, H = lax.axis_size("segment"), lax.axis_size("ctx"), lax.axis_size("head")
    rows, q_cols = queries.shape
    span, kv_cols = keys.shape
    kv_count = kv_cols // HEAD_DIM
    depth, d = out_weight.shape
    width = d // (C * H)
    half = rows // 2
    stat_rows = -(-2 * (depth // HEAD_DIM) // 8) * 8
    whole = pl.BlockSpec(memory_space=pl.ANY)
    scalars = pl.BlockSpec(memory_space=pltpu.SMEM)
    wire = jnp.bfloat16
    return pl.pallas_call(
        functools.partial(relay, (S, C, H)),
        out_shape=jax.ShapeDtypeStruct((rows, width), jnp.bfloat16),
        in_specs=[scalars, scalars, whole, whole, whole, whole],
        out_specs=pl.BlockSpec(memory_space=pltpu.VMEM),
        scratch_shapes=[
            pltpu.VMEM((rows, q_cols), queries.dtype),
            pltpu.VMEM((kv_count, span, HEAD_DIM), keys.dtype),
            pltpu.VMEM((kv_count, span, HEAD_DIM), values.dtype),
            pltpu.VMEM((depth, d), out_weight.dtype),
            pltpu.VMEM((8, span), jnp.float32),
            pltpu.VMEM((2, C, half, depth), wire),
            pltpu.VMEM((2, C - 1, half, depth), wire),
            pltpu.VMEM((2, C, stat_rows, HEAD_DIM), jnp.float32),
            pltpu.VMEM((2, C - 1, stat_rows, HEAD_DIM), jnp.float32),
            pltpu.VMEM((2, half, depth), wire),
            pltpu.VMEM((2, H - 1, C, half, width), wire),
            pltpu.VMEM((2, H - 1, C, half, width), wire),
            pltpu.VMEM((2, C, half, width), wire),
            pltpu.VMEM((2, C, half, width), wire),
            pltpu.SemaphoreType.DMA((2,)),
            pltpu.SemaphoreType.DMA((kv_count,)),
            pltpu.SemaphoreType.DMA((kv_count,)),
            pltpu.SemaphoreType.DMA((2, 2, C - 1)),
            pltpu.SemaphoreType.DMA((2, 2, C - 1)),
            pltpu.SemaphoreType.DMA((2, 2, H - 1, C)),
            pltpu.SemaphoreType.DMA((2, 2, C)),
        ],
        compiler_params=pltpu.CompilerParams(
            collective_id=0, has_side_effects=True, vmem_limit_bytes=58 * 2**20
        ),
        cost_estimate=pl.CostEstimate(
            flops=4 * rows * q_cols * span + 2 * rows * depth * d,
            bytes_accessed=2 * (rows * q_cols + 2 * span * kv_cols + depth * d),
            transcendentals=rows * q_cols // HEAD_DIM * span,
        ),
    )(lengths, selected, queries, keys, values, out_weight)


def solution(mesh):
    placed = (
        P("segment", "head"),
        P(("segment", "ctx"), "head"),
        P(("segment", "ctx"), "head"),
        P("segment"),
        P("segment", None),
        P(("head", "ctx"), None),
    )
    return jax.shard_map(
        on_device,
        mesh=mesh,
        in_specs=placed,
        out_specs=P("segment", ("head", "ctx")),
        check_vma=False,
    )
```

```python
import functools
import math

import jax
import jax.numpy as jnp
from jax import lax
from jax.experimental import pallas as pl
from jax.experimental.pallas import tpu as pltpu
from jax.sharding import PartitionSpec as P

HEAD_DIM = 128
BLOCK = 2048
MASKED = -1e30
FLOOR = -1e20
UNITS = math.log2(math.e) / math.sqrt(HEAD_DIM)
MESH = pl.DeviceIdType.MESH


def relay(
    sizes,
    length_ref,
    chosen_ref,
    q_hbm,
    k_hbm,
    v_hbm,
    w_hbm,
    out_ref,
    q_buf,
    k_buf,
    v_buf,
    w_buf,
    bias,
    a_send,
    a_recv,
    t_send,
    t_recv,
    attn,
    y_send,
    y_recv,
    z_send,
    z_recv,
    load_sem,
    k_sem,
    v_sem,
    a_sems,
    t_sems,
    y_sems,
    z_sems,
):
    S, C, H = sizes
    seg, ctx, head = lax.axis_index("segment"), lax.axis_index("ctx"), lax.axis_index("head")
    rows, q_cols = q_buf.shape
    kv_count, span, _ = k_buf.shape
    per_ctx = q_cols // (HEAD_DIM * C)
    group = q_cols // (HEAD_DIM * kv_count)
    together = math.gcd(per_ctx, 4)
    half = rows // 2
    width = out_ref.shape[1]
    stat_rows = t_send.shape[2]
    aligned = kv_count == C

    barrier = pltpu.get_barrier_semaphore()

    def greet(s, c, h):
        pl.semaphore_signal(barrier, inc=1, device_id=(s, c, h), device_id_type=MESH)

    for k in range(1, C):
        greet(seg, lax.rem(ctx + k, C), head)
    for k in range(1, H):
        greet(seg, ctx, lax.rem(head + k, H))
    for k in range(C):
        greet(lax.rem(seg + S - 1, S), lax.rem(ctx + k, C), head)

    def load_q():
        return pltpu.make_async_copy(q_hbm, q_buf, load_sem.at[0])

    def load_w():
        return pltpu.make_async_copy(w_hbm, w_buf, load_sem.at[1])

    def load_kv(i):
        which = lax.rem(ctx + 1 + i, C) if aligned else i
        columns = pl.ds(pl.multiple_of(which * HEAD_DIM, HEAD_DIM), HEAD_DIM)
        return (
            pltpu.make_async_copy(k_hbm.at[:, columns], k_buf.at[i], k_sem.at[i]),
            pltpu.make_async_copy(v_hbm.at[:, columns], v_buf.at[i], v_sem.at[i]),
        )

    load_q().start()
    for i in range(kv_count):
        for copy in load_kv(i):
            copy.start()
    load_w().start()

    length = length_ref[0]
    for b in range(span // BLOCK):
        first = ctx * span + b * BLOCK
        picked = jnp.int32(0)
        for i in range(chosen_ref.shape[1]):
            picked = jnp.where(chosen_ref[0, i] == first // BLOCK, 1, picked)
        limit = jnp.where(picked == 1, length, 0)
        place = first + lax.broadcasted_iota(jnp.int32, (8, BLOCK), 1)
        bias[:, b * BLOCK : (b + 1) * BLOCK] = jnp.where(place < limit, 0.0, MASKED)

    load_q().wait()
    if not aligned:
        for i in range(kv_count):
            for copy in load_kv(i):
                copy.wait()

    def a_copies(g, k):
        to = (seg, lax.rem(ctx + 1 + k, C), head)
        return (
            pltpu.make_async_remote_copy(
                src_ref=a_send.at[g, k], dst_ref=a_recv.at[g, k], send_sem=a_sems.at[0, g, k],
                recv_sem=a_sems.at[1, g, k], device_id=to, device_id_type=MESH,
            ),
            pltpu.make_async_remote_copy(
                src_ref=t_send.at[g, k], dst_ref=t_recv.at[g, k], send_sem=t_sems.at[0, g, k],
                recv_sem=t_sems.at[1, g, k], device_id=to, device_id_type=MESH,
            ),
        )

    lane = lax.broadcasted_iota(jnp.int32, (half, HEAD_DIM), 1)

    def unit(g, k):
        owner = lax.rem(ctx + 1 + k, C)
        slot = k if aligned else (owner * per_ctx) // group
        own_rows = pl.ds(pl.multiple_of(g * half, half), half)
        tiles = per_ctx // together
        chunk = 2 * HEAD_DIM
        pieces = [slice(first, first + chunk) for first in range(0, span, chunk)]

        def rows_of(t):
            return jnp.concatenate(
                [
                    q_buf[
                        own_rows,
                        pl.ds(
                            pl.multiple_of(
                                (owner * per_ctx + t * together + i) * HEAD_DIM, HEAD_DIM
                            ),
                            HEAD_DIM,
                        ),
                    ]
                    for i in range(together)
                ],
                axis=0,
            )

        def score(q, high, piece):
            block = bias[0:1, piece] + lax.dot_general(
                q, k_buf[slot, piece, :], (((1,), (1,)), ((), ())),
                preferred_element_type=jnp.float32,
            )
            for first in range(0, chunk, HEAD_DIM):
                high = jnp.maximum(high, block[:, first : first + HEAD_DIM])
            return high, block

        floor = jnp.full((together * half, HEAD_DIM), FLOOR, jnp.float32)
        q, high, blocks = rows_of(0), floor, []
        for piece in pieces:
            high, block = score(q, high, piece)
            blocks.append(block)
        stats = jnp.zeros((half, HEAD_DIM), jnp.float32)
        for t in range(tiles):
            top = jnp.max(high, axis=1, keepdims=True)
            level = top * UNITS
            later, expos = [], []
            if t + 1 < tiles:
                q, high = rows_of(t + 1), floor
            for piece, block in zip(pieces, blocks):
                if t + 1 < tiles:
                    high, ahead = score(q, high, piece)
                    later.append(ahead)
                expos.append(jnp.exp2(block * UNITS - level).astype(jnp.bfloat16))
            blocks = later
            ones = jnp.ones((span, HEAD_DIM), jnp.bfloat16)
            summed = jnp.dot(
                jnp.concatenate(expos, axis=1),
                jnp.concatenate([v_buf[slot], ones], axis=1),
                preferred_element_type=jnp.float32,
            )
            for i in range(together):
                part = slice(i * half, (i + 1) * half)
                j = t * together + i
                a_send[g, k, :, j * HEAD_DIM : (j + 1) * HEAD_DIM] = summed[
                    part, :HEAD_DIM
                ].astype(jnp.bfloat16)
                stats = jnp.where(lane == j, top[part], stats)
                stats = jnp.where(lane == per_ctx + j, summed[part, HEAD_DIM:], stats)
        fill = jnp.zeros((HEAD_DIM - half, HEAD_DIM), jnp.float32)
        t_send[g, k] = jnp.transpose(jnp.concatenate([stats, fill], axis=0))[:stat_rows]

    def column_form(block):
        fill = jnp.zeros((HEAD_DIM - stat_rows, HEAD_DIM), jnp.float32)
        return jnp.transpose(jnp.concatenate([block, fill], axis=0))[:half]

    def combine(g):
        for k in range(C - 1):
            for copy in a_copies(g, k):
                copy.wait()
        stats = [column_form(t_recv[g, k]) for k in range(C - 1)]
        stats.append(column_form(t_send[g, C - 1]))
        tops = [s[:, :per_ctx] for s in stats]
        sums = [s[:, per_ctx : 2 * per_ctx] for s in stats]
        largest = functools.reduce(jnp.maximum, tops)
        factors = [jnp.exp2((top - largest) * UNITS) for top in tops]
        total = functools.reduce(jnp.add, [f * s for f, s in zip(factors, sums)])
        factors = [f / total for f in factors]
        for j in range(per_ctx):
            part = slice(j * HEAD_DIM, (j + 1) * HEAD_DIM)
            shares = [a_recv[g, k, :, part] for k in range(C - 1)] + [a_send[g, C - 1, :, part]]
            joined = functools.reduce(
                jnp.add,
                [f[:, j : j + 1] * share.astype(jnp.float32) for f, share in zip(factors, shares)],
            )
            attn[g, :, part] = joined.astype(jnp.bfloat16)

    def columns_of(g, h, k):
        c = lax.rem(ctx + 1 + k, C)
        start = pl.multiple_of((h * C + c) * width, width)
        return jnp.dot(attn[g], w_buf[:, pl.ds(start, width)], preferred_element_type=jnp.float32)

    def y_copy(g, i, k):
        return pltpu.make_async_remote_copy(
            src_ref=y_send.at[g, i, k], dst_ref=y_recv.at[g, i, k], send_sem=y_sems.at[0, g, i, k],
            recv_sem=y_sems.at[1, g, i, k], device_id=(seg, ctx, lax.rem(head + 1 + i, H)),
            device_id_type=MESH,
        )

    def z_copy(g, k):
        return pltpu.make_async_remote_copy(
            src_ref=z_send.at[g, k], dst_ref=z_recv.at[g, k], send_sem=z_sems.at[0, g, k],
            recv_sem=z_sems.at[1, g, k],
            device_id=(lax.rem(seg + 1, S), lax.rem(ctx + 1 + k, C), head),
            device_id_type=MESH,
        )

    def outgoing(g):
        def step(n, carry):
            k, i = n // (H - 1), n % (H - 1)
            y_send[g, i, k] = columns_of(g, lax.rem(head + 1 + i, H), k).astype(jnp.bfloat16)
            y_copy(g, i, k).start()
            return carry

        lax.fori_loop(0, C * (H - 1), step, 0)

    def pass_on(g, first, last):
        def step(k, carry):
            mine = columns_of(g, head, k)
            for i in range(H - 1):
                y_copy(g, i, k).wait()
                mine = mine + y_recv[g, i, k].astype(jnp.float32)
            z_send[g, k] = mine.astype(jnp.bfloat16)
            z_copy(g, k).start()
            return carry

        lax.fori_loop(first, last, step, 0)

    def turn(n, carry):
        g, k = n // C, n % C
        if aligned:

            @pl.when(n < C)
            def _():
                for copy in load_kv(k):
                    copy.wait()

        unit(g, k)

        @pl.when(n == 0)
        def _():
            pl.semaphore_wait(barrier, 2 * C + H - 2)

        @pl.when(k < C - 1)
        def _():
            for copy in a_copies(g, k):
                copy.start()

        @pl.when(n == C)
        def _():
            load_w().wait()
            combine(0)
            outgoing(0)

        @pl.when(n > C)
        def _():
            pass_on(0, (k - 1) * C // (C - 1), k * C // (C - 1))

        return carry

    lax.fori_loop(0, 2 * C, turn, 0)
    combine(1)
    outgoing(1)
    pass_on(1, 0, C)

    for g in range(2):
        result = jnp.zeros((half, width), jnp.float32)
        for k in range(C):
            z_copy(g, k).wait()
            result = result + z_recv[g, k].astype(jnp.float32)
        out_ref[g * half : (g + 1) * half, :] = result.astype(out_ref.dtype)


def on_device(queries, keys, values, lengths, selected, out_weight):
    S, C, H = lax.axis_size("segment"), lax.axis_size("ctx"), lax.axis_size("head")
    rows, q_cols = queries.shape
    span, kv_cols = keys.shape
    kv_count = kv_cols // HEAD_DIM
    depth, d = out_weight.shape
    width = d // (C * H)
    half = rows // 2
    stat_rows = -(-2 * (depth // HEAD_DIM) // 8) * 8
    whole = pl.BlockSpec(memory_space=pl.ANY)
    scalars = pl.BlockSpec(memory_space=pltpu.SMEM)
    wire = jnp.bfloat16
    return pl.pallas_call(
        functools.partial(relay, (S, C, H)),
        out_shape=jax.ShapeDtypeStruct((rows, width), jnp.bfloat16),
        in_specs=[scalars, scalars, whole, whole, whole, whole],
        out_specs=pl.BlockSpec(memory_space=pltpu.VMEM),
        scratch_shapes=[
            pltpu.VMEM((rows, q_cols), queries.dtype),
            pltpu.VMEM((kv_count, span, HEAD_DIM), keys.dtype),
            pltpu.VMEM((kv_count, span, HEAD_DIM), values.dtype),
            pltpu.VMEM((depth, d), out_weight.dtype),
            pltpu.VMEM((8, span), jnp.float32),
            pltpu.VMEM((2, C, half, depth), wire),
            pltpu.VMEM((2, C - 1, half, depth), wire),
            pltpu.VMEM((2, C, stat_rows, HEAD_DIM), jnp.float32),
            pltpu.VMEM((2, C - 1, stat_rows, HEAD_DIM), jnp.float32),
            pltpu.VMEM((2, half, depth), wire),
            pltpu.VMEM((2, H - 1, C, half, width), wire),
            pltpu.VMEM((2, H - 1, C, half, width), wire),
            pltpu.VMEM((2, C, half, width), wire),
            pltpu.VMEM((2, C, half, width), wire),
            pltpu.SemaphoreType.DMA((2,)),
            pltpu.SemaphoreType.DMA((kv_count,)),
            pltpu.SemaphoreType.DMA((kv_count,)),
            pltpu.SemaphoreType.DMA((2, 2, C - 1)),
            pltpu.SemaphoreType.DMA((2, 2, C - 1)),
            pltpu.SemaphoreType.DMA((2, 2, H - 1, C)),
            pltpu.SemaphoreType.DMA((2, 2, C)),
        ],
        compiler_params=pltpu.CompilerParams(
            collective_id=0, has_side_effects=True, vmem_limit_bytes=58 * 2**20
        ),
        cost_estimate=pl.CostEstimate(
            flops=4 * rows * q_cols * span + 2 * rows * depth * d,
            bytes_accessed=2 * (rows * q_cols + 2 * span * kv_cols + depth * d),
            transcendentals=rows * q_cols // HEAD_DIM * span,
        ),
    )(lengths, selected, queries, keys, values, out_weight)


def solution(mesh):
    placed = (
        P("segment", "head"),
        P(("segment", "ctx"), "head"),
        P(("segment", "ctx"), "head"),
        P("segment"),
        P("segment", None),
        P(("head", "ctx"), None),
    )
    return jax.shard_map(
        on_device,
        mesh=mesh,
        in_specs=placed,
        out_specs=P("segment", ("head", "ctx")),
        check_vma=False,
    )
```

```python
import functools
import math

import jax
import jax.numpy as jnp
from jax import lax
from jax.experimental import pallas as pl
from jax.experimental.pallas import tpu as pltpu
from jax.sharding import PartitionSpec as P

HEAD_DIM = 128
BLOCK = 2048
MASKED = -1e30
FLOOR = -1e20
UNITS = math.log2(math.e) / math.sqrt(HEAD_DIM)
MESH = pl.DeviceIdType.MESH


def relay(
    sizes,
    length_ref,
    chosen_ref,
    q_hbm,
    k_hbm,
    v_hbm,
    w_hbm,
    out_ref,
    q_buf,
    k_buf,
    v_buf,
    w_buf,
    bias,
    a_send,
    a_recv,
    t_send,
    t_recv,
    attn,
    y_send,
    y_recv,
    z_send,
    z_recv,
    load_sem,
    k_sem,
    v_sem,
    a_sems,
    t_sems,
    y_sems,
    z_sems,
):
    S, C, H = sizes
    seg, ctx, head = lax.axis_index("segment"), lax.axis_index("ctx"), lax.axis_index("head")
    rows, q_cols = q_buf.shape
    kv_count, span, _ = k_buf.shape
    per_ctx = q_cols // (HEAD_DIM * C)
    group = q_cols // (HEAD_DIM * kv_count)
    together = math.gcd(per_ctx, 8)
    half = rows // 2
    width = out_ref.shape[1]
    stat_rows = t_send.shape[2]
    aligned = kv_count == C

    barrier = pltpu.get_barrier_semaphore()

    def greet(s, c, h):
        pl.semaphore_signal(barrier, inc=1, device_id=(s, c, h), device_id_type=MESH)

    for k in range(1, C):
        greet(seg, lax.rem(ctx + k, C), head)
    for k in range(1, H):
        greet(seg, ctx, lax.rem(head + k, H))
    for k in range(C):
        greet(lax.rem(seg + S - 1, S), lax.rem(ctx + k, C), head)

    def load_q():
        return pltpu.make_async_copy(q_hbm, q_buf, load_sem.at[0])

    def load_w():
        return pltpu.make_async_copy(w_hbm, w_buf, load_sem.at[1])

    def load_kv(i):
        which = lax.rem(ctx + 1 + i, C) if aligned else i
        columns = pl.ds(pl.multiple_of(which * HEAD_DIM, HEAD_DIM), HEAD_DIM)
        return (
            pltpu.make_async_copy(k_hbm.at[:, columns], k_buf.at[i], k_sem.at[i]),
            pltpu.make_async_copy(v_hbm.at[:, columns], v_buf.at[i], v_sem.at[i]),
        )

    load_q().start()
    for i in range(kv_count):
        for copy in load_kv(i):
            copy.start()
    load_w().start()

    length = length_ref[0]
    for b in range(span // BLOCK):
        first = ctx * span + b * BLOCK
        picked = jnp.int32(0)
        for i in range(chosen_ref.shape[1]):
            picked = jnp.where(chosen_ref[0, i] == first // BLOCK, 1, picked)
        limit = jnp.where(picked == 1, length, 0)
        place = first + lax.broadcasted_iota(jnp.int32, (8, BLOCK), 1)
        bias[:, b * BLOCK : (b + 1) * BLOCK] = jnp.where(place < limit, 0.0, MASKED)

    load_q().wait()
    if not aligned:
        for i in range(kv_count):
            for copy in load_kv(i):
                copy.wait()

    def a_copies(g, k):
        to = (seg, lax.rem(ctx + 1 + k, C), head)
        return (
            pltpu.make_async_remote_copy(
                src_ref=a_send.at[g, k], dst_ref=a_recv.at[g, k], send_sem=a_sems.at[0, g, k],
                recv_sem=a_sems.at[1, g, k], device_id=to, device_id_type=MESH,
            ),
            pltpu.make_async_remote_copy(
                src_ref=t_send.at[g, k], dst_ref=t_recv.at[g, k], send_sem=t_sems.at[0, g, k],
                recv_sem=t_sems.at[1, g, k], device_id=to, device_id_type=MESH,
            ),
        )

    lane = lax.broadcasted_iota(jnp.int32, (half, HEAD_DIM), 1)

    def unit(g, k):
        owner = lax.rem(ctx + 1 + k, C)
        slot = k if aligned else (owner * per_ctx) // group
        own_rows = pl.ds(pl.multiple_of(g * half, half), half)
        tiles = per_ctx // together
        scores = []
        for t in range(tiles):
            q = jnp.concatenate(
                [
                    q_buf[
                        own_rows,
                        pl.ds(
                            pl.multiple_of(
                                (owner * per_ctx + t * together + i) * HEAD_DIM, HEAD_DIM
                            ),
                            HEAD_DIM,
                        ),
                    ]
                    for i in range(together)
                ],
                axis=0,
            )
            scores.append(
                lax.dot_general(
                    q, k_buf[slot], (((1,), (1,)), ((), ())), preferred_element_type=jnp.float32
                )
                + bias[0:1, :]
            )
        stats = jnp.zeros((half, HEAD_DIM), jnp.float32)
        for t in range(tiles):
            top = jnp.maximum(jnp.max(scores[t], axis=1, keepdims=True), FLOOR)
            expo = jnp.exp2(scores[t] * UNITS - top * UNITS).astype(jnp.bfloat16)
            ones = jnp.ones((span, HEAD_DIM), jnp.bfloat16)
            summed = jnp.dot(
                expo,
                jnp.concatenate([v_buf[slot], ones], axis=1),
                preferred_element_type=jnp.float32,
            )
            for i in range(together):
                part = slice(i * half, (i + 1) * half)
                j = t * together + i
                a_send[g, k, :, j * HEAD_DIM : (j + 1) * HEAD_DIM] = summed[
                    part, :HEAD_DIM
                ].astype(jnp.bfloat16)
                stats = jnp.where(lane == j, top[part], stats)
                stats = jnp.where(lane == per_ctx + j, summed[part, HEAD_DIM:], stats)
        fill = jnp.zeros((HEAD_DIM - half, HEAD_DIM), jnp.float32)
        t_send[g, k] = jnp.transpose(jnp.concatenate([stats, fill], axis=0))[:stat_rows]

    def column_form(block):
        fill = jnp.zeros((HEAD_DIM - stat_rows, HEAD_DIM), jnp.float32)
        return jnp.transpose(jnp.concatenate([block, fill], axis=0))[:half]

    def combine(g):
        for k in range(C - 1):
            for copy in a_copies(g, k):
                copy.wait()
        stats = [column_form(t_recv[g, k]) for k in range(C - 1)]
        stats.append(column_form(t_send[g, C - 1]))
        tops = [s[:, :per_ctx] for s in stats]
        sums = [s[:, per_ctx : 2 * per_ctx] for s in stats]
        largest = functools.reduce(jnp.maximum, tops)
        factors = [jnp.exp2((top - largest) * UNITS) for top in tops]
        total = functools.reduce(jnp.add, [f * s for f, s in zip(factors, sums)])
        factors = [f / total for f in factors]
        for j in range(per_ctx):
            part = slice(j * HEAD_DIM, (j + 1) * HEAD_DIM)
            shares = [a_recv[g, k, :, part] for k in range(C - 1)] + [a_send[g, C - 1, :, part]]
            joined = functools.reduce(
                jnp.add,
                [f[:, j : j + 1] * share.astype(jnp.float32) for f, share in zip(factors, shares)],
            )
            attn[g, :, part] = joined.astype(jnp.bfloat16)

    def columns_of(g, h, k):
        c = lax.rem(ctx + 1 + k, C)
        start = pl.multiple_of((h * C + c) * width, width)
        return jnp.dot(attn[g], w_buf[:, pl.ds(start, width)], preferred_element_type=jnp.float32)

    def y_copy(g, i, k):
        return pltpu.make_async_remote_copy(
            src_ref=y_send.at[g, i, k], dst_ref=y_recv.at[g, i, k], send_sem=y_sems.at[0, g, i, k],
            recv_sem=y_sems.at[1, g, i, k], device_id=(seg, ctx, lax.rem(head + 1 + i, H)),
            device_id_type=MESH,
        )

    def z_copy(g, k):
        return pltpu.make_async_remote_copy(
            src_ref=z_send.at[g, k], dst_ref=z_recv.at[g, k], send_sem=z_sems.at[0, g, k],
            recv_sem=z_sems.at[1, g, k],
            device_id=(lax.rem(seg + 1, S), lax.rem(ctx + 1 + k, C), head),
            device_id_type=MESH,
        )

    def outgoing(g):
        def step(n, carry):
            k, i = n // (H - 1), n % (H - 1)
            y_send[g, i, k] = columns_of(g, lax.rem(head + 1 + i, H), k).astype(jnp.bfloat16)
            y_copy(g, i, k).start()
            return carry

        lax.fori_loop(0, C * (H - 1), step, 0)

    def pass_on(g, first, last):
        def step(k, carry):
            mine = columns_of(g, head, k)
            for i in range(H - 1):
                y_copy(g, i, k).wait()
                mine = mine + y_recv[g, i, k].astype(jnp.float32)
            z_send[g, k] = mine.astype(jnp.bfloat16)
            z_copy(g, k).start()
            return carry

        lax.fori_loop(first, last, step, 0)

    def turn(n, carry):
        g, k = n // C, n % C
        if aligned:

            @pl.when(n < C)
            def _():
                for copy in load_kv(k):
                    copy.wait()

        unit(g, k)

        @pl.when(n == 0)
        def _():
            pl.semaphore_wait(barrier, 2 * C + H - 2)

        @pl.when(k < C - 1)
        def _():
            for copy in a_copies(g, k):
                copy.start()

        @pl.when(n == C)
        def _():
            load_w().wait()
            combine(0)
            outgoing(0)

        @pl.when(n > C)
        def _():
            pass_on(0, (k - 1) * C // (C - 1), k * C // (C - 1))

        return carry

    lax.fori_loop(0, 2 * C, turn, 0)
    combine(1)
    outgoing(1)
    pass_on(1, 0, C)

    for g in range(2):
        result = jnp.zeros((half, width), jnp.float32)
        for k in range(C):
            z_copy(g, k).wait()
            result = result + z_recv[g, k].astype(jnp.float32)
        out_ref[g * half : (g + 1) * half, :] = result.astype(out_ref.dtype)


def on_device(queries, keys, values, lengths, selected, out_weight):
    S, C, H = lax.axis_size("segment"), lax.axis_size("ctx"), lax.axis_size("head")
    rows, q_cols = queries.shape
    span, kv_cols = keys.shape
    kv_count = kv_cols // HEAD_DIM
    depth, d = out_weight.shape
    width = d // (C * H)
    half = rows // 2
    stat_rows = -(-2 * (depth // HEAD_DIM) // 8) * 8
    whole = pl.BlockSpec(memory_space=pl.ANY)
    scalars = pl.BlockSpec(memory_space=pltpu.SMEM)
    wire = jnp.bfloat16
    return pl.pallas_call(
        functools.partial(relay, (S, C, H)),
        out_shape=jax.ShapeDtypeStruct((rows, width), jnp.bfloat16),
        in_specs=[scalars, scalars, whole, whole, whole, whole],
        out_specs=pl.BlockSpec(memory_space=pltpu.VMEM),
        scratch_shapes=[
            pltpu.VMEM((rows, q_cols), queries.dtype),
            pltpu.VMEM((kv_count, span, HEAD_DIM), keys.dtype),
            pltpu.VMEM((kv_count, span, HEAD_DIM), values.dtype),
            pltpu.VMEM((depth, d), out_weight.dtype),
            pltpu.VMEM((8, span), jnp.float32),
            pltpu.VMEM((2, C, half, depth), wire),
            pltpu.VMEM((2, C - 1, half, depth), wire),
            pltpu.VMEM((2, C, stat_rows, HEAD_DIM), jnp.float32),
            pltpu.VMEM((2, C - 1, stat_rows, HEAD_DIM), jnp.float32),
            pltpu.VMEM((2, half, depth), wire),
            pltpu.VMEM((2, H - 1, C, half, width), wire),
            pltpu.VMEM((2, H - 1, C, half, width), wire),
            pltpu.VMEM((2, C, half, width), wire),
            pltpu.VMEM((2, C, half, width), wire),
            pltpu.SemaphoreType.DMA((2,)),
            pltpu.SemaphoreType.DMA((kv_count,)),
            pltpu.SemaphoreType.DMA((kv_count,)),
            pltpu.SemaphoreType.DMA((2, 2, C - 1)),
            pltpu.SemaphoreType.DMA((2, 2, C - 1)),
            pltpu.SemaphoreType.DMA((2, 2, H - 1, C)),
            pltpu.SemaphoreType.DMA((2, 2, C)),
        ],
        compiler_params=pltpu.CompilerParams(
            collective_id=0, has_side_effects=True, vmem_limit_bytes=58 * 2**20
        ),
        cost_estimate=pl.CostEstimate(
            flops=4 * rows * q_cols * span + 2 * rows * depth * d,
            bytes_accessed=2 * (rows * q_cols + 2 * span * kv_cols + depth * d),
            transcendentals=rows * q_cols // HEAD_DIM * span,
        ),
    )(lengths, selected, queries, keys, values, out_weight)


def solution(mesh):
    placed = (
        P("segment", "head"),
        P(("segment", "ctx"), "head"),
        P(("segment", "ctx"), "head"),
        P("segment"),
        P("segment", None),
        P(("head", "ctx"), None),
    )
    return jax.shard_map(
        on_device,
        mesh=mesh,
        in_specs=placed,
        out_specs=P("segment", ("head", "ctx")),
        check_vma=False,
    )
```
